32 devices in a mesh: groups: 2 (over x), expert: 2 (over core), blk: 8 (over z, y).
Axes of the slice: x: 2, y: 2, z: 4, core: 2. Of those that a mesh axis runs over, the one named last changes fastest.
Arguments:
- residual: bfloat16 [640, 6144], P(('groups', 'expert', 'blk')), parts along dimension 0, may hold values from -6 to 6
- queries: bfloat16 [640, 6144], P(('groups', 'expert', 'blk')), parts along dimension 0, may hold values from -6 to 6
- keys: bfloat16 [640, 32, 1024], P(('groups', 'expert', 'blk')), parts along dimension 0, may hold values from -6 to 6
- values: bfloat16 [640, 32, 1024], P(('groups', 'expert', 'blk')), parts along dimension 0, may hold values from -6 to 6
- lengths: int32 [640], P(('groups', 'expert', 'blk')), parts along dimension 0, may hold values from 2 to 32, as said below
- norm_gain: float32 [6144], replicated, may hold values from 0.5 to 1.5
- routes: int32 [640, 2], P(('groups', 'expert', 'blk')), parts along dimension 0, may hold values from 0 to 7, as said below
- gate_scores: float32 [640, 2], P(('groups', 'expert', 'blk')), parts along dimension 0, may hold values from 0.25 to 4
- w_gate: bfloat16 [2, 6144, 8192], P('expert', None, 'blk'), may hold values from -0.078125 to 0.078125
- w_up: bfloat16 [2, 6144, 8192], P('expert', None, 'blk'), may hold values from -0.078125 to 0.078125
- w_down: bfloat16 [2, 8192, 6144], P('expert', 'blk'), may hold values from -0.0625 to 0.0625
Outputs:
- mixed: bfloat16 [640, 6144], P(('groups', 'expert', 'blk')), parts along dimension 0
The draws below stay inside these ranges and needn't reach their ends.
There are 2 independent parts, one for each index of `groups`. The reference program is written for one: setup_inputs(seed, part) draws one part's arguments, and reference() takes and returns one part's arrays. A program takes and returns all parts, laid end to end along the dimension named above; an argument that names none is the same for every part. Nothing has to cross between parts.
Inputs may be any that keep to these rules, and one draw needn't show every extreme that they name: `routes`: each request names two different experts. In the requests of one aligned block of 20, no expert is named by more than 6; one expert below 2 is named by exactly 6 in every block. `lengths`: some request has exactly 32 live positions.
All inputs are finite; a program needn't handle non-finite values.
Results may differ from the reference program's by a relative error of at most 0.005.
Values may be sent and summed in bfloat16 or wider, within the bound.
A program may use at most 128 MiB of HBM per device.

```python
import math
import jax
import jax.numpy as jnp
from jax import lax

D = 6144
HEADS = 48
KV_HEADS = 8
HEAD_DIM = 128
ALL_EXPERTS = 8
FF = 8192
TOP = 2
ROW_DEV = 20
LEN = 32
CAP = 6
EXPERTS = 2
ROWS = 320
N_EXPERT = 2
N_BLK = 8


def draw_queries(key, part):
    key = jax.random.fold_in(key, 11)
    base = jnp.clip(jax.random.normal(key, (ROWS, HEADS * HEAD_DIM), jnp.float32), -6.0, 6.0)
    return base.astype(jnp.bfloat16)


def draw_keys(key, part):
    key = jax.random.fold_in(key, 12)
    base = jnp.clip(jax.random.normal(key, (ROWS, LEN, KV_HEADS * HEAD_DIM), jnp.float32), -6.0, 6.0)
    return base.astype(jnp.bfloat16)


def draw_lengths(key, part):
    key = jax.random.fold_in(key, 13)
    drawn = jax.random.randint(key, (ROWS,), 2, LEN + 1, dtype=jnp.int32)
    return drawn.at[0].set(LEN)


def draw_routes(key, part):
    key = jax.random.fold_in(key, 14)
    block_count = ROWS // ROW_DEV
    key_full, key_order, key_offset = jax.random.split(key, 3)
    full_expert = jax.random.randint(key_full, (), 0, EXPERTS, dtype=jnp.int32)
    ranking = jax.random.randint(key_order, (block_count, ALL_EXPERTS), 0, 1 << 20, dtype=jnp.int32) * ALL_EXPERTS
    ranking = ranking + jnp.arange(ALL_EXPERTS, dtype=jnp.int32)[None, :]
    ordering = jnp.argsort(ranking, axis=1).astype(jnp.int32)
    leading = ordering[:, :1]
    ordering = jnp.where(ordering == full_expert, leading, ordering)
    ordering = ordering.at[:, 0].set(full_expert)
    offsets = jax.random.randint(key_offset, (block_count,), 5, 8, dtype=jnp.int32)
    lanes = jnp.arange(ROW_DEV, dtype=jnp.int32)
    first_index = jnp.broadcast_to((lanes % ALL_EXPERTS)[None, :], (block_count, ROW_DEV))
    second_index = (lanes[None, :] + offsets[:, None]) % ALL_EXPERTS
    first_pick = jnp.take_along_axis(ordering, first_index, axis=1)
    second_pick = jnp.take_along_axis(ordering, second_index, axis=1)
    return jnp.stack([first_pick, second_pick], axis=-1).reshape(ROWS, TOP).astype(jnp.int32)


def steps_of(key, dims, shards, low, top_value):
    factor_of, own = 1.0, jax.random.fold_in(key, 6)
    for axis_at, shards_of in shards:
        draws = jnp.exp(jax.random.uniform(jax.random.fold_in(own, axis_at), (shards_of,), jnp.float32, low / len(shards), top_value / len(shards)))
        factor_of = factor_of * jnp.repeat(draws, dims[axis_at] // shards_of).reshape([-1 if axis == axis_at else 1 for axis in range(len(dims))])
    return factor_of


def scatter_about(key, shape, scale, most, pieces=(), kind=jnp.bfloat16):
    loudness = steps_of(key, shape, pieces, -0.22, 0.18) if pieces else 1.0
    result = jax.random.normal(key, shape, jnp.float32) * scale * loudness
    return jnp.minimum(jnp.maximum(result, -most), most).astype(kind)


def setup_inputs(seed: int = 0, part: int = 0) -> dict:
    key_list = jax.random.split(jax.random.key(seed), 12)
    own_keys = jax.random.split(jax.random.fold_in(key_list[11], part), 12)
    return {
        "residual": scatter_about(own_keys[0], (ROWS, D), 1.0, 6.0, ((0, 16),)),
        "queries": draw_queries(jax.random.fold_in(jax.random.fold_in(key_list[11], part), 71), part),
        "keys": draw_keys(jax.random.fold_in(jax.random.fold_in(key_list[11], part), 71), part),
        "values": scatter_about(own_keys[3], (ROWS, LEN, KV_HEADS * HEAD_DIM), 1.0, 6.0, ((0, 16),)),
        "lengths": draw_lengths(jax.random.fold_in(jax.random.fold_in(key_list[11], part), 71), part),
        "norm_gain": jnp.clip(1.0 + 0.1 * jax.random.normal(key_list[5], (D,), jnp.float32), 0.5, 1.5),
        "routes": draw_routes(jax.random.fold_in(jax.random.fold_in(key_list[11], part), 71), part),
        "gate_scores": jnp.clip(jnp.exp(math.log(4.0) - 2.7725887 * jax.random.uniform(own_keys[7], (ROWS, TOP), jnp.float32) ** steps_of(own_keys[7], (ROWS, TOP), ((0, 16),), -0.2, 0.2)), 0.25, 4.0),
        "w_gate": scatter_about(key_list[8], (EXPERTS, D, FF), D ** -0.5, 0.078125, ((0, 2), (2, 8))),
        "w_up": scatter_about(key_list[9], (EXPERTS, D, FF), D ** -0.5, 0.078125, ((0, 2), (2, 8))),
        "w_down": scatter_about(key_list[10], (EXPERTS, FF, D), FF ** -0.5, 0.0625, ((0, 2), (1, 8))),
    }


def down_sum(activated, down_weight):
    range_width = FF // N_BLK
    total = jnp.zeros((activated.shape[0], D), jnp.float32)
    for range_id in range(N_BLK):
        low = range_id * range_width
        partial_value = jnp.dot(activated[:, low:low + range_width], down_weight[low:low + range_width], preferred_element_type=jnp.float32).astype(jnp.bfloat16)
        partial_value = lax.optimization_barrier(partial_value)
        total = total + partial_value.astype(jnp.float32)
    return total

def reference(residual, queries, keys, values, lengths, norm_gain, routes, gate_scores, w_gate, w_up, w_down):
    row_count = residual.shape[0]
    group_size = HEADS // KV_HEADS
    query_heads = queries.astype(jnp.float32).reshape(row_count, KV_HEADS, group_size, HEAD_DIM)
    key_heads = keys.astype(jnp.float32).reshape(row_count, LEN, KV_HEADS, HEAD_DIM)
    value_heads = values.astype(jnp.float32).reshape(row_count, LEN, KV_HEADS, HEAD_DIM)
    scores = jnp.einsum('rgjd,rtgd->rgjt', query_heads, key_heads) * HEAD_DIM ** (-0.5)
    position = jnp.arange(LEN, dtype=jnp.int32)
    valid_mask = position[None, :] < lengths[:, None]
    scores = jnp.where(valid_mask[:, None, None, :], scores, jnp.float32(-1e+30))
    top_score = lax.optimization_barrier(jnp.max(scores, axis=-1, keepdims=True))
    exponent = jnp.exp(scores - top_score)
    attn_probs = (exponent / lax.optimization_barrier(jnp.sum(exponent, axis=-1, keepdims=True))).astype(jnp.bfloat16)
    attended = jnp.einsum('rgjt,rtgd->rgjd', attn_probs.astype(jnp.float32), value_heads).reshape(row_count, D)
    hidden_state = residual.astype(jnp.float32) + attended
    mean_square = lax.optimization_barrier(jnp.mean(hidden_state * hidden_state, axis=1, keepdims=True))
    normed_rows = (hidden_state * lax.rsqrt(mean_square + 1e-05) * norm_gain[None, :]).astype(jnp.bfloat16)
    chosen = routes[:, :, None] == jnp.arange(EXPERTS, dtype=jnp.int32)[None, None, :]
    membership = lax.optimization_barrier(jnp.sum(chosen.astype(jnp.int32), axis=1)).astype(jnp.int32)
    gate_weights = gate_scores / lax.optimization_barrier(jnp.sum(gate_scores, axis=1, keepdims=True))
    expert_weight = lax.optimization_barrier(jnp.sum(gate_weights[:, :, None] * chosen.astype(jnp.float32), axis=1))
    device_count = N_EXPERT * N_BLK
    blocked = membership.reshape(device_count, ROW_DEV, EXPERTS)
    earlier = (jnp.cumsum(blocked, axis=1) - blocked).reshape(row_count, EXPERTS).astype(jnp.int32)
    owner = (jnp.arange(row_count, dtype=jnp.int32) // ROW_DEV).astype(jnp.int32)
    slot_index = jnp.where(membership > 0, owner[:, None] * CAP + earlier, device_count * CAP).astype(jnp.int32)
    total = hidden_state
    for expert_id in range(EXPERTS):
        slot_buffer = jnp.zeros((device_count * CAP, D), jnp.bfloat16).at[slot_index[:, expert_id]].set(normed_rows, mode='drop')
        gate_part = jnp.dot(slot_buffer, w_gate[expert_id], preferred_element_type=jnp.float32)
        up_part = jnp.dot(slot_buffer, w_up[expert_id], preferred_element_type=jnp.float32)
        activated = (jax.nn.silu(gate_part) * up_part).astype(jnp.bfloat16)
        section_output = down_sum(activated, w_down[expert_id]).astype(jnp.bfloat16)
        picked = section_output[jnp.minimum(slot_index[:, expert_id], device_count * CAP - 1)].astype(jnp.float32)
        total = total + expert_weight[:, expert_id:expert_id + 1] * picked
    return total.astype(jnp.bfloat16)
```

```python
import functools

import jax
import jax.numpy as jnp
from jax import lax
from jax.experimental import pallas as pl
from jax.experimental.pallas import tpu as pltpu
from jax.sharding import PartitionSpec as P

HEADS = 48
KV_HEADS = 8
HEAD_DIM = 128
GROUP = HEADS // KV_HEADS
CAP = 6
PIECE = 16
LIVE = 2 * CAP
CHUNK = 1024
QUARTER = CHUNK // 4
PACK = 3 * QUARTER
PAD = 24
TILE = 128
MESH = pl.DeviceIdType.MESH


def f32_dot(a, b):
    return jnp.dot(a, b, preferred_element_type=jnp.float32)


def kernel(
    n, residual, queries, meta, gain, keys, values, w_gate, w_up, w_down, mixed,
    kbuf, vbuf, wg, wu, wd, qs, hid, live,
    osend, inbox, gath, xfull, gacc, uacc, act,
    part, ybuf, red, zbuf, fin, pfin,
    kv_sem, wg_sem, wu_sem, wd_sem,
    i_sems, z_sems, y_sems, ry_sems, rz_sems, ri_sems,
):
    rows = residual.shape[0]
    width = residual.shape[1]
    cache_len = keys.shape[1]
    chunks = width // CHUNK
    units = wg.shape[1]
    unit_tile = min(units, QUARTER)
    nc = n // 2
    total = n * PIECE
    core = lax.axis_index("expert")
    me = lax.axis_index("blk")
    yc = lax.rem(me, 2)
    zc = lax.div(me, 2)
    other = 1 - core
    y_partner = me + 1 - 2 * yc

    def column_peer(k):
        return lax.rem(zc + k, nc) * 2 + yc

    barrier = pltpu.get_barrier_semaphore()
    pl.semaphore_signal(barrier, inc=1, device_id={"expert": other}, device_id_type=MESH)
    pl.semaphore_signal(barrier, inc=1, device_id={"blk": y_partner}, device_id_type=MESH)
    for k in range(1, nc):
        pl.semaphore_signal(barrier, inc=1, device_id={"blk": column_peer(k)}, device_id_type=MESH)

    key_copy = pltpu.make_async_copy(keys, kbuf, kv_sem.at[0])
    value_copy = pltpu.make_async_copy(values, vbuf, kv_sem.at[1])
    key_copy.start()
    value_copy.start()

    def chunk_at(c):
        return pl.ds(pl.multiple_of(c * CHUNK, CHUNK), CHUNK)

    def gate_copy(c):
        return pltpu.make_async_copy(w_gate.at[0, chunk_at(c)], wg.at[chunk_at(c)], wg_sem.at[c])

    def up_copy(c):
        return pltpu.make_async_copy(w_up.at[0, chunk_at(c)], wu.at[chunk_at(c)], wu_sem.at[c])

    def down_copy(c):
        return pltpu.make_async_copy(w_down.at[0, :, chunk_at(c)], wd.at[c], wd_sem.at[c])

    @pl.loop(0, chunks)
    def _(c):
        gate_copy(c).start()
        up_copy(c).start()

    @pl.loop(0, chunks)
    def _(c):
        down_copy(c).start()

    row_id = lax.broadcasted_iota(jnp.int32, (PAD, TILE), 0)
    lane_id = lax.broadcasted_iota(jnp.int32, (PAD, TILE), 1)

    def as_column(row):
        return jnp.sum(jnp.where(row_id == lane_id, row, 0.0), axis=1, keepdims=True)

    first, second = meta[0:1, :], meta[1:2, :]
    score0, score1 = meta[2:3, :], meta[3:4, :]
    lengths = as_column(meta[4:5, :])
    slot_row = lax.broadcasted_iota(jnp.int32, (PIECE, TILE), 0).astype(jnp.float32)
    slot_lane = lax.broadcasted_iota(jnp.int32, (PAD, PIECE), 1).astype(jnp.float32)
    base = (core * CAP).astype(jnp.float32)

    def tables(expert):
        wanted = expert.astype(jnp.float32)
        in_first, in_second = first == wanted, second == wanted
        member = jnp.where(in_first, 1.0, 0.0) + jnp.where(in_second, 1.0, 0.0)
        gate = (jnp.where(in_first, score0, 0.0) + jnp.where(in_second, score1, 0.0)) / (
            score0 + score1
        )
        member_column = as_column(member)
        earlier = jnp.sum(jnp.where(row_id < lane_id, member_column, 0.0), axis=0, keepdims=True)
        slot = jnp.where(member > 0, earlier + base, -100.0)
        slot_column = as_column(slot)
        send = [jnp.where((slot_row == slot) & (slot_row < LIVE), 1.0, 0.0)]
        take = [jnp.where((slot_lane == slot_column) & (slot_lane < LIVE), 1.0, 0.0)]
        for i in range(3):
            send.append(
                jnp.where((slot_row + (4 * i - LIVE) == slot) & (slot_row >= LIVE), 1.0, 0.0)
            )
            take.append(
                jnp.where(
                    (slot_lane + (4 * i - LIVE) == slot_column) & (slot_lane >= LIVE), 1.0, 0.0
                )
            )
        return (
            [s[:, :PAD] for s in send],
            [t.astype(jnp.bfloat16) for t in take],
            as_column(gate),
        )

    send_own, take_own, gate_own = tables(core)
    send_other, take_other, gate_other = tables(other)
    send_main = jnp.concatenate([send_own[0], send_other[0]], axis=0).astype(jnp.bfloat16)
    send_tail = jnp.concatenate(
        [t for i in range(1, 4) for t in (send_own[i], send_other[i])], axis=0
    ).astype(jnp.bfloat16)

    place = lax.broadcasted_iota(jnp.int32, live.shape, 1) - cache_len * lax.broadcasted_iota(
        jnp.int32, live.shape, 0
    )
    place = place.astype(jnp.float32)
    live[...] = jnp.where((place >= 0) & (place < lengths), 1.0, 0.0)
    tail = (PAD - 16, width)
    qs[16:PAD, :] = jnp.zeros(tail, jnp.float32)
    hid[16:PAD, :] = jnp.zeros(tail, jnp.float32)
    qs[0:rows, :] = queries[...].astype(jnp.float32)
    hid[0:rows, :] = residual[...].astype(jnp.float32)
    key_copy.wait()
    value_copy.wait()

    def head(g, squares):
        def cols(j):
            return pl.ds(pl.multiple_of((g * GROUP + j) * HEAD_DIM, HEAD_DIM), HEAD_DIM)

        kv_cols = pl.ds(pl.multiple_of(g * HEAD_DIM, HEAD_DIM), HEAD_DIM)
        q = jnp.concatenate([qs[:, cols(j)] for j in range(GROUP)], axis=0).astype(jnp.bfloat16)
        k = kbuf[:, :, kv_cols].reshape(rows * cache_len, HEAD_DIM)
        v = vbuf[:, :, kv_cols].reshape(rows * cache_len, HEAD_DIM)
        scores = lax.dot_general(
            q, k, (((1,), (1,)), ((), ())), preferred_element_type=jnp.float32
        ) * HEAD_DIM ** (-0.5)
        scores = scores.reshape(GROUP, PAD, rows * cache_len)
        scores = jnp.where(live[...][None] > 0, scores, -1e30)
        exponent = jnp.exp(scores - jnp.max(scores, axis=-1, keepdims=True))
        probs = exponent / jnp.sum(exponent, axis=-1, keepdims=True)
        probs = probs.reshape(GROUP * PAD, rows * cache_len).astype(jnp.bfloat16)
        attended = f32_dot(probs, v)
        for j in range(GROUP):
            h = hid[:, cols(j)] + attended[j * PAD:(j + 1) * PAD]
            hid[:, cols(j)] = h
            squares = squares + h * h
        return squares

    squares = lax.fori_loop(0, KV_HEADS, head, jnp.zeros((PAD, HEAD_DIM), jnp.float32))
    inverse = lax.rsqrt(jnp.sum(squares, axis=1, keepdims=True) * (1.0 / width) + 1e-5)

    def in_chip(c):
        return pltpu.make_async_remote_copy(
            osend.at[c], inbox.at[c], i_sems.at[0, c], i_sems.at[1, c],
            device_id={"expert": other}, device_id_type=MESH,
        )

    def along_column(c, k):
        mine = gath.at[c, yc, zc]
        return pltpu.make_async_remote_copy(
            mine, mine, z_sems.at[0, c, k - 1], z_sems.at[1, c, k - 1],
            device_id={"blk": column_peer(k)}, device_id_type=MESH,
        )

    def from_column(c, k):
        theirs = gath.at[c, yc, lax.rem(zc + nc - k, nc)]
        return pltpu.make_async_remote_copy(
            theirs, theirs, z_sems.at[0, c, k - 1], z_sems.at[1, c, k - 1],
            device_id={"blk": column_peer(k)}, device_id_type=MESH,
        )

    def to_partner(c, y):
        column = gath.at[c, y]
        return pltpu.make_async_remote_copy(
            column, column, y_sems.at[0, c], y_sems.at[1, c],
            device_id={"blk": y_partner}, device_id_type=MESH,
        )

    pl.semaphore_wait(barrier, nc + 1)

    @pl.loop(0, chunks)
    def _(c):
        at = chunk_at(c)
        normed = (hid[:, at] * inverse * gain[:, at]).astype(jnp.bfloat16)
        main = f32_dot(send_main, normed[:, :PACK])
        last = f32_dot(send_tail, normed[:, PACK:])
        both = 2 * PIECE
        packed = main + jnp.concatenate([last[i * both:(i + 1) * both] for i in range(3)], axis=1)
        packed = packed.astype(jnp.bfloat16)
        gath[c, yc, zc] = packed[:PIECE]
        osend[c] = packed[PIECE:]
        in_chip(c).start()

    @pl.loop(0, chunks)
    def _(c):
        in_chip(c).wait_recv()
        gath[c, yc, zc] = (
            gath[c, yc, zc].astype(jnp.float32) + inbox[c].astype(jnp.float32)
        ).astype(jnp.bfloat16)
        for k in range(1, nc):
            along_column(c, k).start()

    span_a = lax.broadcasted_iota(jnp.int32, (TILE, TILE), 0)
    span_b = lax.broadcasted_iota(jnp.int32, (TILE, TILE), 1)
    in_piece = span_a & (PIECE - 1)
    spread, collect = [], []
    for i in range(3):
        spread.append(
            jnp.where(
                (span_b == span_a + (LIVE - 4 * i)) & (in_piece >= 4 * i) & (in_piece < 4 * i + 4),
                1.0, 0.0,
            )
        )
        collect.append(
            jnp.where((span_b == span_a - (LIVE - 4 * i)) & (in_piece >= LIVE), 1.0, 0.0)
        )
    spread = jnp.concatenate(spread, axis=1).astype(jnp.bfloat16)
    collect = jnp.concatenate(collect, axis=0).astype(jnp.bfloat16)
    groups = [slice(t, t + TILE) for t in range(0, total, TILE)]

    gacc[...] = jnp.zeros(gacc.shape, jnp.float32)
    uacc[...] = jnp.zeros(uacc.shape, jnp.float32)

    @pl.loop(0, chunks + 1)
    def _(s):
        @pl.when(s < chunks)
        def _():
            for k in range(1, nc):
                from_column(s, k).wait_recv()
            to_partner(s, yc).start()

        @pl.when(s > 0)
        def _():
            c = s - 1
            to_partner(c, 1 - yc).wait_recv()
            packed = gath[c].reshape(total, PACK)
            xfull[:, :PACK] = packed
            for group in groups:
                stacked = jnp.concatenate(
                    [packed[group, i * QUARTER:(i + 1) * QUARTER] for i in range(3)], axis=0
                )
                xfull[group, PACK:] = f32_dot(spread, stacked).astype(jnp.bfloat16)
            gate_copy(c).wait()
            up_copy(c).wait()

            @pl.loop(0, units // unit_tile)
            def _(t):
                tile = pl.ds(pl.multiple_of(t * unit_tile, unit_tile), unit_tile)
                x = xfull[...]
                gacc[:, tile] += f32_dot(x, wg[chunk_at(c), tile])
                uacc[:, tile] += f32_dot(x, wu[chunk_at(c), tile])

    @pl.loop(0, units // unit_tile)
    def _(t):
        tile = pl.ds(pl.multiple_of(t * unit_tile, unit_tile), unit_tile)
        g = gacc[:, tile]
        act[:, tile] = (g / (1.0 + jnp.exp(-g)) * uacc[:, tile]).astype(jnp.bfloat16)

    def sum_partner(c):
        return pltpu.make_async_remote_copy(
            part.at[c, 1 - yc], ybuf.at[c], ry_sems.at[0, c], ry_sems.at[1, c],
            device_id={"blk": y_partner}, device_id_type=MESH,
        )

    def sum_column(c, k):
        return pltpu.make_async_remote_copy(
            red.at[c, lax.rem(zc + k, nc)], zbuf.at[c, k - 1],
            rz_sems.at[0, c, k - 1], rz_sems.at[1, c, k - 1],
            device_id={"blk": column_peer(k)}, device_id_type=MESH,
        )

    def swap(c):
        return pltpu.make_async_remote_copy(
            fin.at[c], pfin.at[c], ri_sems.at[0, c], ri_sems.at[1, c],
            device_id={"expert": other}, device_id_type=MESH,
        )

    live_row = (lax.broadcasted_iota(jnp.int32, (total, QUARTER), 0) & (PIECE - 1)) < LIVE

    @pl.loop(0, chunks + 3)
    def _(s):
        @pl.when(s < chunks)
        def _():
            down_copy(s).wait()
            a = act[...]
            last = f32_dot(a, wd[s, :, PACK:]).astype(jnp.bfloat16)
            moved = [f32_dot(collect, last[group]) for group in groups]
            for i in range(3):
                y = f32_dot(a, wd[s, :, i * QUARTER:(i + 1) * QUARTER])
                extra = jnp.concatenate([m[i * TILE:(i + 1) * TILE] for m in moved], axis=0)
                packed = jnp.where(live_row, y, extra).astype(jnp.bfloat16)
                part[s, :, :, :, i * QUARTER:(i + 1) * QUARTER] = packed.reshape(
                    2, nc, PIECE, QUARTER
                )
            sum_partner(s).start()

        @pl.when((s >= 1) & (s <= chunks))
        def _():
            c = s - 1
            sum_partner(c).wait_recv()
            red[c] = (
                part[c, yc].astype(jnp.float32) + ybuf[c].astype(jnp.float32)
            ).astype(jnp.bfloat16)
            for k in range(1, nc):
                sum_column(c, k).start()

        @pl.when((s >= 2) & (s <= chunks + 1))
        def _():
            c = s - 2
            for k in range(1, nc):
                sum_column(c, k).wait_recv()
            value = red[c, zc].astype(jnp.float32)
            for k in range(1, nc):
                value = value + zbuf[c, k - 1].astype(jnp.float32)
            fin[c] = value.astype(jnp.bfloat16)
            swap(c).start()

        @pl.when(s >= 3)
        def _():
            c = s - 3
            swap(c).wait_recv()
            main = hid[:, pl.ds(pl.multiple_of(c * CHUNK, CHUNK), PACK)]
            last = hid[:, pl.ds(pl.multiple_of(c * CHUNK + PACK, QUARTER), QUARTER)]
            for take, gate, outs in (
                (take_own, gate_own, fin[c]), (take_other, gate_other, pfin[c])
            ):
                main = main + gate * f32_dot(take[0], outs)
                picked = f32_dot(take[1], outs[:, :QUARTER])
                for i in range(1, 3):
                    picked = picked + f32_dot(
                        take[i + 1], outs[:, i * QUARTER:(i + 1) * QUARTER]
                    )
                last = last + gate * picked
            mixed[:, pl.ds(pl.multiple_of(c * CHUNK, CHUNK), PACK)] = main[:rows].astype(
                jnp.bfloat16
            )
            mixed[:, pl.ds(pl.multiple_of(c * CHUNK + PACK, QUARTER), QUARTER)] = last[
                :rows
            ].astype(jnp.bfloat16)

    @pl.loop(0, chunks)
    def _(c):
        in_chip(c).wait_send()
        to_partner(c, yc).wait_send()
        sum_partner(c).wait_send()
        swap(c).wait_send()
        for k in range(1, nc):
            along_column(c, k).wait_send()
            sum_column(c, k).wait_send()


def on_device(
    residual, queries, keys, values, lengths, norm_gain, routes, gate_scores, w_gate, w_up, w_down
):
    n = lax.axis_size("blk")
    nc = n // 2
    rows, width = residual.shape
    cache_len = keys.shape[1]
    units = w_gate.shape[2]
    chunks = width // CHUNK
    total = n * PIECE
    meta = jnp.pad(
        jnp.concatenate(
            [routes.T.astype(jnp.float32), gate_scores.T, lengths[None].astype(jnp.float32)], axis=0
        ),
        ((0, 3), (0, TILE - rows)),
        constant_values=-1.0,
    )
    bf16, f32 = jnp.bfloat16, jnp.float32
    vmem = pl.BlockSpec(memory_space=pltpu.VMEM)
    anywhere = pl.BlockSpec(memory_space=pl.ANY)
    dma = pltpu.SemaphoreType.DMA
    return pl.pallas_call(
        functools.partial(kernel, n),
        out_shape=jax.ShapeDtypeStruct((rows, width), bf16),
        in_specs=[vmem] * 4 + [anywhere] * 5,
        out_specs=vmem,
        scratch_shapes=[
            pltpu.VMEM(keys.shape, bf16),
            pltpu.VMEM(values.shape, bf16),
            pltpu.VMEM((width, units), bf16),
            pltpu.VMEM((width, units), bf16),
            pltpu.VMEM((chunks, units, CHUNK), bf16),
            pltpu.VMEM((PAD, width), f32),
            pltpu.VMEM((PAD, width), f32),
            pltpu.VMEM((PAD, rows * cache_len), f32),
            pltpu.VMEM((chunks, PIECE, PACK), bf16),
            pltpu.VMEM((chunks, PIECE, PACK), bf16),
            pltpu.VMEM((chunks, 2, nc, PIECE, PACK), bf16),
            pltpu.VMEM((total, CHUNK), bf16),
            pltpu.VMEM((total, units), f32),
            pltpu.VMEM((total, units), f32),
            pltpu.VMEM((total, units), bf16),
            pltpu.VMEM((chunks, 2, nc, PIECE, PACK), bf16),
            pltpu.VMEM((chunks, nc, PIECE, PACK), bf16),
            pltpu.VMEM((chunks, nc, PIECE, PACK), bf16),
            pltpu.VMEM((chunks, nc - 1, PIECE, PACK), bf16),
            pltpu.VMEM((chunks, PIECE, PACK), bf16),
            pltpu.VMEM((chunks, PIECE, PACK), bf16),
            dma((2,)),
            dma((chunks,)),
            dma((chunks,)),
            dma((chunks,)),
            dma((2, chunks)),
            dma((2, chunks, nc - 1)),
            dma((2, chunks)),
            dma((2, chunks)),
            dma((2, chunks, nc - 1)),
            dma((2, chunks)),
        ],
        compiler_params=pltpu.CompilerParams(
            collective_id=0, has_side_effects=True, vmem_limit_bytes=60 * 1024 * 1024
        ),
    )(residual, queries, meta, norm_gain.reshape(1, width), keys, values, w_gate, w_up, w_down)


def solution(mesh):
    return jax.shard_map(
        on_device,
        mesh=mesh,
        in_specs=(
            P(("groups", "expert", "blk"), None),
            P(("groups", "expert", "blk"), None),
            P(("groups", "expert", "blk"), None, None),
            P(("groups", "expert", "blk"), None, None),
            P(("groups", "expert", "blk")),
            P(),
            P(("groups", "expert", "blk"), None),
            P(("groups", "expert", "blk"), None),
            P("expert", None, "blk"),
            P("expert", None, "blk"),
            P("expert", "blk", None),
        ),
        out_specs=P(("groups", "expert", "blk"), None),
        check_vma=False,
    )
```

```python
import functools

import jax
import jax.numpy as jnp
from jax import lax
from jax.experimental import pallas as pl
from jax.experimental.pallas import tpu as pltpu
from jax.sharding import PartitionSpec as P

HEADS = 48
KV_HEADS = 8
HEAD_DIM = 128
GROUP = HEADS // KV_HEADS
CAP = 6
PIECE = 16
LIVE = 2 * CAP
CHUNK = 1024
QUARTER = CHUNK // 4
PACK = 3 * QUARTER
PAD = 24
TILE = 128
MESH = pl.DeviceIdType.MESH


def f32_dot(a, b):
    return jnp.dot(a, b, preferred_element_type=jnp.float32)


def kernel(
    n, residual, queries, routes, scores_in, lengths_in, gain, keys, values, w_gate, w_up, w_down, mixed,
    kbuf, vbuf, wg, wu, wd, qs, hid, live, meta, sc, pr,
    osend, inbox, gath, xfull, gacc, uacc, act,
    part, ybuf, red, zbuf, fin, pfin,
    kv_sem, wg_sem, wu_sem, wd_sem,
    i_sems, z_sems, y_sems, ry_sems, rz_sems, ri_sems,
):
    rows = residual.shape[0]
    width = residual.shape[1]
    cache_len = keys.shape[1]
    chunks = width // CHUNK
    units = wg.shape[1]
    unit_tile = min(units, QUARTER)
    nc = n // 2
    total = n * PIECE
    core = lax.axis_index("expert")
    me = lax.axis_index("blk")
    yc = lax.rem(me, 2)
    zc = lax.div(me, 2)
    other = 1 - core
    y_partner = me + 1 - 2 * yc

    def column_peer(k):
        return lax.rem(zc + k, nc) * 2 + yc

    barrier = pltpu.get_barrier_semaphore()
    pl.semaphore_signal(barrier, inc=1, device_id={"expert": other}, device_id_type=MESH)
    pl.semaphore_signal(barrier, inc=1, device_id={"blk": y_partner}, device_id_type=MESH)
    for k in range(1, nc):
        pl.semaphore_signal(barrier, inc=1, device_id={"blk": column_peer(k)}, device_id_type=MESH)

    key_copy = pltpu.make_async_copy(keys, kbuf, kv_sem.at[0])
    value_copy = pltpu.make_async_copy(values, vbuf, kv_sem.at[1])
    key_copy.start()
    value_copy.start()

    def chunk_at(c):
        return pl.ds(pl.multiple_of(c * CHUNK, CHUNK), CHUNK)

    def gate_copy(c):
        return pltpu.make_async_copy(w_gate.at[0, chunk_at(c)], wg.at[chunk_at(c)], wg_sem.at[c])

    def up_copy(c):
        return pltpu.make_async_copy(w_up.at[0, chunk_at(c)], wu.at[chunk_at(c)], wu_sem.at[c])

    def down_copy(c):
        return pltpu.make_async_copy(w_down.at[0, :, chunk_at(c)], wd.at[c], wd_sem.at[c])

    @pl.loop(0, chunks)
    def _(c):
        gate_copy(c).start()
        up_copy(c).start()

    @pl.loop(0, chunks)
    def _(c):
        down_copy(c).start()

    row_id = lax.broadcasted_iota(jnp.int32, (PAD, TILE), 0)
    lane_id = lax.broadcasted_iota(jnp.int32, (PAD, TILE), 1)

    def as_column(row):
        return jnp.sum(jnp.where(row_id == lane_id, row, 0.0), axis=1, keepdims=True)

    meta[...] = jnp.full(meta.shape, -1.0, jnp.float32)
    meta[0:2, 0:rows] = routes[...].astype(jnp.float32)
    meta[2:4, 0:rows] = scores_in[...]
    meta[4:5, 0:rows] = lengths_in[...].astype(jnp.float32)
    first, second = meta[0:1, :], meta[1:2, :]
    score0, score1 = meta[2:3, :], meta[3:4, :]
    lengths = as_column(meta[4:5, :])
    slot_row = lax.broadcasted_iota(jnp.int32, (PIECE, TILE), 0).astype(jnp.float32)
    slot_lane = lax.broadcasted_iota(jnp.int32, (PAD, PIECE), 1).astype(jnp.float32)
    base = (core * CAP).astype(jnp.float32)

    def tables(expert):
        wanted = expert.astype(jnp.float32)
        in_first, in_second = first == wanted, second == wanted
        member = jnp.where(in_first, 1.0, 0.0) + jnp.where(in_second, 1.0, 0.0)
        gate = (jnp.where(in_first, score0, 0.0) + jnp.where(in_second, score1, 0.0)) / (
            score0 + score1
        )
        member_column = as_column(member)
        earlier = jnp.sum(jnp.where(row_id < lane_id, member_column, 0.0), axis=0, keepdims=True)
        slot = jnp.where(member > 0, earlier + base, -100.0)
        slot_column = as_column(slot)
        send = [jnp.where((slot_row == slot) & (slot_row < LIVE), 1.0, 0.0)]
        take = [jnp.where((slot_lane == slot_column) & (slot_lane < LIVE), 1.0, 0.0)]
        for i in range(3):
            send.append(
                jnp.where((slot_row + (4 * i - LIVE) == slot) & (slot_row >= LIVE), 1.0, 0.0)
            )
            take.append(
                jnp.where(
                    (slot_lane + (4 * i - LIVE) == slot_column) & (slot_lane >= LIVE), 1.0, 0.0
                )
            )
        return (
            [s[:, :PAD] for s in send],
            [t.astype(jnp.bfloat16) for t in take],
            as_column(gate),
        )

    send_own, take_own, gate_own = tables(core)
    send_other, take_other, gate_other = tables(other)
    send_main = jnp.concatenate([send_own[0], send_other[0]], axis=0).astype(jnp.bfloat16)
    send_tail = jnp.concatenate(
        [t for i in range(1, 4) for t in (send_own[i], send_other[i])], axis=0
    ).astype(jnp.bfloat16)

    place = lax.broadcasted_iota(jnp.int32, live.shape, 1) - cache_len * lax.broadcasted_iota(
        jnp.int32, live.shape, 0
    )
    place = place.astype(jnp.float32)
    live[...] = jnp.where((place >= 0) & (place < lengths), 1.0, 0.0)
    tail = (PAD - 16, width)
    qs[16:PAD, :] = jnp.zeros(tail, jnp.float32)
    hid[16:PAD, :] = jnp.zeros(tail, jnp.float32)
    qs[0:rows, :] = queries[...].astype(jnp.float32)
    hid[0:rows, :] = residual[...].astype(jnp.float32)
    key_copy.wait()
    value_copy.wait()

    batches = [(start, min(8, rows - start)) for start in range(0, rows, 8)]

    def key_products(g, _):
        for start, held in batches:
            span = slice(start * cache_len, (start + held) * cache_len)
            q = jnp.concatenate([qs[start:start + 8, head_cols(g, j)] for j in range(GROUP)], axis=0)
            k = kbuf[start:start + held, :, kv_cols(g)].reshape(held * cache_len, HEAD_DIM)
            sc[g, :, span] = lax.dot_general(
                q.astype(jnp.bfloat16), k, (((1,), (1,)), ((), ())),
                preferred_element_type=jnp.float32,
            ) * HEAD_DIM ** (-0.5)
        return _

    def head_cols(g, j):
        return pl.ds(pl.multiple_of((g * GROUP + j) * HEAD_DIM, HEAD_DIM), HEAD_DIM)

    def kv_cols(g):
        return pl.ds(pl.multiple_of(g * HEAD_DIM, HEAD_DIM), HEAD_DIM)

    def softmax(g, _):
        for start, held in batches:
            span = slice(start * cache_len, (start + held) * cache_len)
            scores = sc[g, :, span].reshape(GROUP, 8, held * cache_len)
            scores = jnp.where(live[start:start + 8, span][None] > 0, scores, -1e30)
            exponent = jnp.exp(scores - jnp.max(scores, axis=-1, keepdims=True))
            probs = exponent * (1.0 / jnp.sum(exponent, axis=-1, keepdims=True))
            pr[g, :, span] = probs.reshape(GROUP * 8, held * cache_len).astype(jnp.bfloat16)
        return _

    def value_products(g, squares):
        sums = []
        for (start, held), square in zip(batches, squares):
            span = slice(start * cache_len, (start + held) * cache_len)
            v = vbuf[start:start + held, :, kv_cols(g)].reshape(held * cache_len, HEAD_DIM)
            attended = f32_dot(pr[g, :, span], v)
            for j in range(GROUP):
                h = hid[start:start + 8, head_cols(g, j)] + attended[j * 8:(j + 1) * 8]
                hid[start:start + 8, head_cols(g, j)] = h
                square = square + h * h
            sums.append(square)
        return tuple(sums)

    lax.fori_loop(0, KV_HEADS, key_products, 0, unroll=8)
    lax.fori_loop(0, KV_HEADS, softmax, 0, unroll=8)
    squares = lax.fori_loop(
        0, KV_HEADS, value_products,
        tuple(jnp.zeros((8, HEAD_DIM), jnp.float32) for _ in batches), unroll=8,
    )
    squares = jnp.concatenate(squares, axis=0)
    inverse = lax.rsqrt(jnp.sum(squares, axis=1, keepdims=True) * (1.0 / width) + 1e-5)

    def in_chip(c):
        return pltpu.make_async_remote_copy(
            osend.at[c], inbox.at[c], i_sems.at[0, c], i_sems.at[1, c],
            device_id={"expert": other}, device_id_type=MESH,
        )

    def along_column(c, k):
        mine = gath.at[c, yc, zc]
        return pltpu.make_async_remote_copy(
            mine, mine, z_sems.at[0, c, k - 1], z_sems.at[1, c, k - 1],
            device_id={"blk": column_peer(k)}, device_id_type=MESH,
        )

    def from_column(c, k):
        theirs = gath.at[c, yc, lax.rem(zc + nc - k, nc)]
        return pltpu.make_async_remote_copy(
            theirs, theirs, z_sems.at[0, c, k - 1], z_sems.at[1, c, k - 1],
            device_id={"blk": column_peer(k)}, device_id_type=MESH,
        )

    def to_partner(c, y, k):
        piece = gath.at[c, y, lax.rem(zc + nc - k, nc)]
        return pltpu.make_async_remote_copy(
            piece, piece, y_sems.at[0, c, k], y_sems.at[1, c, k],
            device_id={"blk": y_partner}, device_id_type=MESH,
        )

    pl.semaphore_wait(barrier, nc + 1)

    @pl.loop(0, chunks)
    def _(c):
        at = chunk_at(c)
        normed = (hid[:, at] * inverse * gain[:, at]).astype(jnp.bfloat16)
        main = f32_dot(send_main, normed[:, :PACK])
        last = f32_dot(send_tail, normed[:, PACK:])
        both = 2 * PIECE
        packed = main + jnp.concatenate([last[i * both:(i + 1) * both] for i in range(3)], axis=1)
        packed = packed.astype(jnp.bfloat16)
        gath[c, yc, zc] = packed[:PIECE]
        osend[c] = packed[PIECE:]
        in_chip(c).start()

    @pl.loop(0, chunks)
    def _(c):
        in_chip(c).wait_recv()
        gath[c, yc, zc] = (
            gath[c, yc, zc].astype(jnp.float32) + inbox[c].astype(jnp.float32)
        ).astype(jnp.bfloat16)
        for k in range(1, nc):
            along_column(c, k).start()
        to_partner(c, yc, 0).start()

    span_a = lax.broadcasted_iota(jnp.int32, (TILE, TILE), 0)
    span_b = lax.broadcasted_iota(jnp.int32, (TILE, TILE), 1)
    in_piece = span_a & (PIECE - 1)
    spread, collect = [], []
    for i in range(3):
        spread.append(
            jnp.where(
                (span_b == span_a + (LIVE - 4 * i)) & (in_piece >= 4 * i) & (in_piece < 4 * i + 4),
                1.0, 0.0,
            )
        )
        collect.append(
            jnp.where((span_b == span_a - (LIVE - 4 * i)) & (in_piece >= LIVE), 1.0, 0.0)
        )
    spread = jnp.concatenate(spread, axis=1).astype(jnp.bfloat16)
    collect = jnp.concatenate(collect, axis=0).astype(jnp.bfloat16)
    groups = [slice(t, t + TILE) for t in range(0, total, TILE)]

    gacc[...] = jnp.zeros(gacc.shape, jnp.float32)
    uacc[...] = jnp.zeros(uacc.shape, jnp.float32)

    @pl.loop(0, chunks + 1)
    def _(s):
        @pl.when(s < chunks)
        def _():
            for k in range(1, nc):
                from_column(s, k).wait_recv()
                to_partner(s, yc, k).start()

        @pl.when(s > 0)
        def _():
            c = s - 1
            for k in range(nc):
                to_partner(c, 1 - yc, k).wait_recv()
            packed = gath[c].reshape(total, PACK)
            xfull[:, :PACK] = packed
            for group in groups:
                stacked = jnp.concatenate(
                    [packed[group, i * QUARTER:(i + 1) * QUARTER] for i in range(3)], axis=0
                )
                xfull[group, PACK:] = f32_dot(spread, stacked).astype(jnp.bfloat16)
            gate_copy(c).wait()
            up_copy(c).wait()

            @pl.loop(0, units // unit_tile)
            def _(t):
                tile = pl.ds(pl.multiple_of(t * unit_tile, unit_tile), unit_tile)
                x = xfull[...]
                gacc[:, tile] += f32_dot(x, wg[chunk_at(c), tile])
                uacc[:, tile] += f32_dot(x, wu[chunk_at(c), tile])

    @pl.loop(0, units // unit_tile)
    def _(t):
        tile = pl.ds(pl.multiple_of(t * unit_tile, unit_tile), unit_tile)
        g = gacc[:, tile]
        act[:, tile] = (g / (1.0 + jnp.exp(-g)) * uacc[:, tile]).astype(jnp.bfloat16)

    def sum_partner(c, k):
        z = lax.rem(zc + k, nc)
        return pltpu.make_async_remote_copy(
            part.at[c, 1 - yc, z], ybuf.at[c, z], ry_sems.at[0, c, k], ry_sems.at[1, c, k],
            device_id={"blk": y_partner}, device_id_type=MESH,
        )

    def sum_column(c, k):
        return pltpu.make_async_remote_copy(
            red.at[c, lax.rem(zc + k, nc)], zbuf.at[c, k - 1],
            rz_sems.at[0, c, k - 1], rz_sems.at[1, c, k - 1],
            device_id={"blk": column_peer(k)}, device_id_type=MESH,
        )

    def swap(c):
        return pltpu.make_async_remote_copy(
            fin.at[c], pfin.at[c], ri_sems.at[0, c], ri_sems.at[1, c],
            device_id={"expert": other}, device_id_type=MESH,
        )

    live_row = (lax.broadcasted_iota(jnp.int32, (total, QUARTER), 0) & (PIECE - 1)) < LIVE

    @pl.loop(0, chunks + 3)
    def _(s):
        @pl.when(s < chunks)
        def _():
            down_copy(s).wait()
            a = act[...]
            last = f32_dot(a, wd[s, :, PACK:]).astype(jnp.bfloat16)
            moved = [f32_dot(collect, last[group]) for group in groups]
            for i in range(3):
                y = f32_dot(a, wd[s, :, i * QUARTER:(i + 1) * QUARTER])
                extra = jnp.concatenate([m[i * TILE:(i + 1) * TILE] for m in moved], axis=0)
                packed = jnp.where(live_row, y, extra).astype(jnp.bfloat16)
                part[s, :, :, :, i * QUARTER:(i + 1) * QUARTER] = packed.reshape(
                    2, nc, PIECE, QUARTER
                )
            for k in (*range(1, nc), 0):
                sum_partner(s, k).start()

        @pl.when((s >= 1) & (s <= chunks))
        def _():
            c = s - 1
            for k in (*range(1, nc), 0):
                sum_partner(c, k).wait_recv()
                z = lax.rem(zc + k, nc)
                red[c, z] = (
                    part[c, yc, z].astype(jnp.float32) + ybuf[c, z].astype(jnp.float32)
                ).astype(jnp.bfloat16)
                if k > 0:
                    sum_column(c, k).start()

        @pl.when((s >= 2) & (s <= chunks + 1))
        def _():
            c = s - 2
            for k in range(1, nc):
                sum_column(c, k).wait_recv()
            value = red[c, zc].astype(jnp.float32)
            for k in range(1, nc):
                value = value + zbuf[c, k - 1].astype(jnp.float32)
            fin[c] = value.astype(jnp.bfloat16)
            swap(c).start()

        @pl.when(s >= 3)
        def _():
            c = s - 3
            swap(c).wait_recv()
            main = hid[:, pl.ds(pl.multiple_of(c * CHUNK, CHUNK), PACK)]
            last = hid[:, pl.ds(pl.multiple_of(c * CHUNK + PACK, QUARTER), QUARTER)]
            for take, gate, outs in (
                (take_own, gate_own, fin[c]), (take_other, gate_other, pfin[c])
            ):
                main = main + gate * f32_dot(take[0], outs)
                picked = f32_dot(take[1], outs[:, :QUARTER])
                for i in range(1, 3):
                    picked = picked + f32_dot(
                        take[i + 1], outs[:, i * QUARTER:(i + 1) * QUARTER]
                    )
                last = last + gate * picked
            mixed[:, pl.ds(pl.multiple_of(c * CHUNK, CHUNK), PACK)] = main[:rows].astype(
                jnp.bfloat16
            )
            mixed[:, pl.ds(pl.multiple_of(c * CHUNK + PACK, QUARTER), QUARTER)] = last[
                :rows
            ].astype(jnp.bfloat16)

    @pl.loop(0, chunks)
    def _(c):
        in_chip(c).wait_send()
        swap(c).wait_send()
        for k in range(nc):
            to_partner(c, yc, k).wait_send()
            sum_partner(c, k).wait_send()
        for k in range(1, nc):
            along_column(c, k).wait_send()
            sum_column(c, k).wait_send()


def on_device(
    residual, queries, keys, values, lengths, norm_gain, routes, gate_scores, w_gate, w_up, w_down
):
    n = lax.axis_size("blk")
    nc = n // 2
    rows, width = residual.shape
    cache_len = keys.shape[1]
    units = w_gate.shape[2]
    chunks = width // CHUNK
    total = n * PIECE
    bf16, f32 = jnp.bfloat16, jnp.float32
    vmem = pl.BlockSpec(memory_space=pltpu.VMEM)
    anywhere = pl.BlockSpec(memory_space=pl.ANY)
    dma = pltpu.SemaphoreType.DMA
    return pl.pallas_call(
        functools.partial(kernel, n),
        out_shape=jax.ShapeDtypeStruct((rows, width), bf16),
        in_specs=[vmem] * 6 + [anywhere] * 5,
        out_specs=vmem,
        scratch_shapes=[
            pltpu.VMEM(keys.shape, bf16),
            pltpu.VMEM(values.shape, bf16),
            pltpu.VMEM((width, units), bf16),
            pltpu.VMEM((width, units), bf16),
            pltpu.VMEM((chunks, units, CHUNK), bf16),
            pltpu.VMEM((PAD, width), f32),
            pltpu.VMEM((PAD, width), f32),
            pltpu.VMEM((PAD, rows * cache_len), f32),
            pltpu.VMEM((8, TILE), f32),
            pltpu.VMEM((KV_HEADS, GROUP * 8, rows * cache_len), f32),
            pltpu.VMEM((KV_HEADS, GROUP * 8, rows * cache_len), bf16),
            pltpu.VMEM((chunks, PIECE, PACK), bf16),
            pltpu.VMEM((chunks, PIECE, PACK), bf16),
            pltpu.VMEM((chunks, 2, nc, PIECE, PACK), bf16),
            pltpu.VMEM((total, CHUNK), bf16),
            pltpu.VMEM((total, units), f32),
            pltpu.VMEM((total, units), f32),
            pltpu.VMEM((total, units), bf16),
            pltpu.VMEM((chunks, 2, nc, PIECE, PACK), bf16),
            pltpu.VMEM((chunks, nc, PIECE, PACK), bf16),
            pltpu.VMEM((chunks, nc, PIECE, PACK), bf16),
            pltpu.VMEM((chunks, nc - 1, PIECE, PACK), bf16),
            pltpu.VMEM((chunks, PIECE, PACK), bf16),
            pltpu.VMEM((chunks, PIECE, PACK), bf16),
            dma((2,)),
            dma((chunks,)),
            dma((chunks,)),
            dma((chunks,)),
            dma((2, chunks)),
            dma((2, chunks, nc - 1)),
            dma((2, chunks, nc)),
            dma((2, chunks, nc)),
            dma((2, chunks, nc - 1)),
            dma((2, chunks)),
        ],
        compiler_params=pltpu.CompilerParams(
            collective_id=0, has_side_effects=True, vmem_limit_bytes=60 * 1024 * 1024
        ),
    )(
        residual, queries, routes.T, gate_scores.T, lengths.reshape(1, rows),
        norm_gain.reshape(1, width), keys, values, w_gate, w_up, w_down,
    )


def solution(mesh):
    return jax.shard_map(
        on_device,
        mesh=mesh,
        in_specs=(
            P(("groups", "expert", "blk"), None),
            P(("groups", "expert", "blk"), None),
            P(("groups", "expert", "blk"), None, None),
            P(("groups", "expert", "blk"), None, None),
            P(("groups", "expert", "blk")),
            P(),
            P(("groups", "expert", "blk"), None),
            P(("groups", "expert", "blk"), None),
            P("expert", None, "blk"),
            P("expert", None, "blk"),
            P("expert", "blk", None),
        ),
        out_specs=P(("groups", "expert", "blk"), None),
        check_vma=False,
    )
```
